32 devices in a mesh: sta: 16 (over z, y, x), pt: 2 (over core).
Axes of the slice: x: 2, y: 2, z: 4, core: 2. Of those that a mesh axis runs over, the one named last changes fastest.
Arguments:
- greens: bfloat16 [2, 64, 1024], P(None, 'sta', 'pt'), may hold values from -6 to 6
- source_power: float32 [1024], P('pt'), may hold values from 0.25 to 4
- observed: float32 [2, 64, 64], P(None, 'sta'), may hold values from -6 to 6
- pair_class: int32 [64, 64], P('sta'), may hold values from 0 to 7
- class_weight: float32 [8], replicated, may hold values from 0.5 to 4
Outputs:
- correlations: float32 [2, 64, 64], P(None, 'sta', 'pt')
- source_gradient: float32 [1024], P('pt')
The draws below stay inside these ranges and needn't reach their ends.
All inputs are finite; a program needn't handle non-finite values.
Results may differ from the reference program's by a relative error of at most 0.0018.
Values may be sent and summed in bfloat16 or wider, within the bound.
A program may use at most 64 MiB of HBM per device.

```python
import math
import jax
import jax.numpy as jnp
from jax import lax

CLASSES = 8
STATIONS = 64
POINTS = 1024


def plant(array, stream_key, smallest, largest):
    index_at = [jax.random.randint(jax.random.fold_in(stream_key, axis), (), 0, length) for axis, length in enumerate(array.shape)]
    widest = array.shape.index(max(array.shape))
    beside = index_at[:widest] + [(index_at[widest] + 1) % array.shape[widest]] + index_at[widest + 1:]
    return array.at[tuple(index_at)].set(smallest).at[tuple(beside)].set(largest)


def levels(rng, dims, pieces, low, high):
    gain = 1.0
    for axis_at, blocks in pieces:
        steps = jax.random.uniform(jax.random.fold_in(jax.random.fold_in(rng, 6), axis_at), (blocks,), jnp.float32, low / len(pieces), high / len(pieces))
        gain = gain * jnp.repeat(jnp.exp(steps), dims[axis_at] // blocks).reshape((-1,) + (1,) * (len(dims) - 1 - axis_at))
    return gain


def centred(rng, extent, width, bound, shards=(), kind=jnp.bfloat16):
    array = jax.random.normal(rng, extent, jnp.float32) * width
    if len(shards) > 0:
        array = levels(rng, extent, shards, -0.22, 0.18) * array
    return jnp.clip(array, min=-bound, max=bound).astype(kind)


def setup_inputs(seed: int = 0) -> dict:
    arg_keys = jax.random.split(jax.random.key(seed), 6)
    return {
        "greens": centred(arg_keys[0], (2, STATIONS, POINTS), 1.0, 6.0, ((1, 16), (2, 2))),
        "source_power": jnp.clip(jnp.exp(math.log(4.0) - 2.7725887 * jax.random.uniform(arg_keys[1], (POINTS,), jnp.float32) ** levels(arg_keys[1], (POINTS,), ((0, 2),), -0.2, 0.2)), 0.25, 4.0),
        "observed": centred(arg_keys[2], (2, STATIONS, STATIONS), 1.0, 6.0, ((1, 16),), jnp.float32),
        "pair_class": plant(jax.random.randint(arg_keys[3], (STATIONS, STATIONS), 0, CLASSES), jax.random.fold_in(arg_keys[3], 1), 0, CLASSES - 1).astype(jnp.int32),
        "class_weight": jnp.clip(jnp.exp(jax.random.uniform(arg_keys[4], (CLASSES,), jnp.float32, math.log(0.5), math.log(4.0))), 0.5, 4.0),
    }


def pair_weights(pair_class, class_weight, rows, cols):
    total = jnp.zeros(pair_class.shape, jnp.float32)
    for level in range(1, CLASSES):
        total = total + jnp.where(pair_class == level, class_weight[level], 0.0).astype(jnp.float32)
    row_ids = jnp.arange(rows, dtype=jnp.int32)[:, None]
    col_ids = jnp.arange(cols, dtype=jnp.int32)[None, :]
    return jnp.where(row_ids == col_ids, 0.0, total).astype(jnp.float32)

def reference(greens, source_power, observed, pair_class, class_weight):
    weighted = (source_power[None, None, :] * greens.astype(jnp.float32)).astype(jnp.bfloat16)
    green_real, green_imag = (greens[0], greens[1])
    left_real, left_imag = (weighted[0], weighted[1])
    scale_pts = 1.0 / math.sqrt(POINTS)
    corr_real = jnp.dot(left_real, green_real.T, preferred_element_type=jnp.float32) + jnp.dot(left_imag, green_imag.T, preferred_element_type=jnp.float32)
    corr_imag = jnp.dot(left_real, green_imag.T, preferred_element_type=jnp.float32) - jnp.dot(left_imag, green_real.T, preferred_element_type=jnp.float32)
    correlations = jnp.stack([corr_real, corr_imag]) * scale_pts
    weights = pair_weights(pair_class, class_weight, STATIONS, STATIONS)
    adjoint = (weights[None] * (correlations - observed)).astype(jnp.bfloat16)
    field_real = jnp.dot(adjoint[0], green_real, preferred_element_type=jnp.float32) + jnp.dot(adjoint[1], green_imag, preferred_element_type=jnp.float32)
    field_imag = jnp.dot(adjoint[0], green_imag, preferred_element_type=jnp.float32) - jnp.dot(adjoint[1], green_real, preferred_element_type=jnp.float32)
    gradient = lax.optimization_barrier(jnp.sum(green_real.astype(jnp.float32) * field_real + green_imag.astype(jnp.float32) * field_imag, axis=0)) / STATIONS
    return (correlations, gradient)
```

```python
import functools
import math

import jax
import jax.numpy as jnp
from jax import lax
from jax.experimental import pallas as pl
from jax.experimental.pallas import tpu as pltpu
from jax.sharding import PartitionSpec as P

CLASSES = 8
MESH = pl.DeviceIdType.MESH
UNROLL = 16


def each(first, last, step):
    if last - first <= UNROLL:
        for i in range(first, last):
            step(i)
    else:
        pl.loop(first, last)(step)


def kernel(
    n, m, greens_ref, power_ref, observed_ref, class_ref, weight_ref, corr_ref, grad_ref,
    greens_v, power_v, observed_v, class_v, weight_s, all_v, field_v, part_v, recv_v, gap_v, pair_v,
    in_sem, send_sem, recv_sem, pt_send, pt_recv,
):
    me, mine = lax.axis_index("sta"), lax.axis_index("pt")
    own, pts = greens_ref.shape[1], greens_ref.shape[2]
    stations = own * n
    half = pts // 2
    rows = 4 * own

    loads = [
        pltpu.make_async_copy(src, dst, in_sem.at[i])
        for i, (src, dst) in enumerate(
            ((greens_ref, greens_v), (observed_ref, observed_v), (class_ref, class_v),
             (power_ref, power_v), (weight_ref, weight_s))
        )
    ]
    for load in loads:
        load.start()

    barrier = pltpu.get_barrier_semaphore()

    def greet(i):
        pl.semaphore_signal(barrier, inc=1, device_id={"sta": lax.rem(me + i, n), "pt": mine}, device_id_type=MESH)

    def greet_pt(i):
        pl.semaphore_signal(barrier, inc=1, device_id={"sta": me, "pt": lax.rem(mine + i, m)}, device_id_type=MESH)

    each(1, n, greet)
    each(1, m, greet_pt)

    for load in loads[:3]:
        load.wait()
    g = greens_v[...].astype(jnp.float32)
    points = jnp.concatenate(
        [g[0, :, :half], g[1, :, :half], g[0, :, half:], g[1, :, half:]], axis=0
    ).astype(jnp.bfloat16)
    obs = jnp.concatenate([observed_v[0], observed_v[1]], axis=1)
    high = obs.astype(jnp.bfloat16).astype(jnp.float32)
    rest = obs - high
    mid = rest.astype(jnp.bfloat16).astype(jnp.float32)
    low = rest - mid
    cls = class_v[...].astype(jnp.float32)
    side = jnp.concatenate([high, mid, low, jnp.concatenate([cls, cls], axis=1)], axis=0).astype(jnp.bfloat16)
    here = all_v.at[pl.ds(pl.multiple_of(me * rows, rows), rows)]
    here[:, :half] = points
    here[:, half:] = side

    pl.semaphore_wait(barrier, (n - 1) + (m - 1))

    def send(i):
        pltpu.make_async_remote_copy(
            src_ref=here, dst_ref=here, send_sem=send_sem, recv_sem=recv_sem,
            device_id={"sta": lax.rem(me + i, n), "pt": mine}, device_id_type=MESH,
        ).start()

    each(1, n, send)

    group = math.gcd(n, 16)
    span = group * own
    size = group * rows
    at = lax.broadcasted_iota(jnp.int32, (size, size), 0)
    of = lax.broadcasted_iota(jnp.int32, (size, size), 1)
    source = (at % span) // own * rows + at // span * own + at % own
    order = jnp.where(of == source, 1.0, 0.0).astype(jnp.bfloat16)
    loads[3].wait()
    loads[4].wait()
    power = [power_v[:, :half], power_v[:, half:]]

    everything = all_v.at[pl.ds(0, (n - 1) * rows)]
    pltpu.make_async_copy(everything, everything, recv_sem).wait()

    def sort(b):
        block = all_v[pl.ds(pl.multiple_of(b * size, size), size), :]
        y = jnp.dot(order, block, preferred_element_type=jnp.float32)
        to = pl.ds(pl.multiple_of(b * span, span), span)
        for q in range(4):
            field_v[q, to, :] = y[q * span:(q + 1) * span, :half].astype(jnp.bfloat16)
        o = y[:, half:]
        gap_v[to, :] = o[:span] + o[span:2 * span] + o[2 * span:3 * span]
        c = o[3 * span:]
        total = jnp.zeros(c.shape, jnp.float32)
        for level in range(1, CLASSES):
            total = jnp.where(c == float(level), weight_s[level], total)
        row_ids = b * span + lax.broadcasted_iota(jnp.int32, c.shape, 0)
        col_ids = lax.broadcasted_iota(jnp.int32, c.shape, 1) % stations
        pair_v[to, :] = jnp.where(row_ids == col_ids, 0.0, total)

    each(0, n // group, sort)

    real, imag = (field_v[0], field_v[2]), (field_v[1], field_v[3])
    right = [
        jnp.concatenate([real[0], imag[0]], axis=0), jnp.concatenate([real[1], imag[1]], axis=0),
        jnp.concatenate([imag[0], -real[0]], axis=0), jnp.concatenate([imag[1], -real[1]], axis=0),
    ]
    right_real = jnp.concatenate([real[0], real[1], imag[0], imag[1]], axis=1)
    right_imag = jnp.concatenate([imag[0], imag[1], -real[0], -real[1]], axis=1)
    rights = jnp.concatenate([right_real, right_imag], axis=0)

    def correlate(b):
        to = pl.ds(pl.multiple_of(b * span, span), span)
        left = jnp.concatenate(
            [
                (power[h] * field_v[2 * h + part, to, :].astype(jnp.float32)).astype(jnp.bfloat16)
                for part in range(2) for h in range(2)
            ],
            axis=1,
        )
        part_v[to, :] = lax.dot_general(left, rights, (((1,), (1,)), ((), ())), preferred_element_type=jnp.float32)

    each(0, n // group, correlate)

    def exchange(i):
        return pltpu.make_async_remote_copy(
            src_ref=part_v, dst_ref=recv_v.at[i - 1], send_sem=pt_send.at[i - 1], recv_sem=pt_recv.at[i - 1],
            device_id={"sta": me, "pt": lax.rem(mine + i, m)}, device_id_type=MESH,
        )

    copies = [exchange(i) for i in range(1, m)]
    for copy in copies:
        copy.start()
    for copy in copies:
        copy.wait_recv()
    for copy in copies:
        copy.wait_send()

    scale = 1.0 / math.sqrt(pts * m)

    def adjoint(b, totals):
        to = pl.ds(pl.multiple_of(b * span, span), span)
        corr = part_v[to, :]
        for i in range(m - 1):
            corr = corr + recv_v[i, to, :]
        corr = corr * scale
        part_v[to, :] = corr
        a = (pair_v[to, :] * (corr - gap_v[to, :])).astype(jnp.bfloat16)
        out = []
        for h in range(2):
            field_real = jnp.dot(a, right[h], preferred_element_type=jnp.float32)
            field_imag = jnp.dot(a, right[2 + h], preferred_element_type=jnp.float32)
            term = (
                field_v[2 * h, to, :].astype(jnp.float32) * field_real
                + field_v[2 * h + 1, to, :].astype(jnp.float32) * field_imag
            )
            out.append(totals[h] + jnp.sum(term, axis=0, keepdims=True))
        return tuple(out)

    zero = jnp.zeros((1, half), jnp.float32)
    if n == group:
        totals = adjoint(0, (zero, zero))
    else:
        totals = lax.fori_loop(0, n // group, adjoint, (zero, zero))
    for h in range(2):
        grad_ref[:, h * half:(h + 1) * half] = totals[h] / stations

    share = stations // m
    tile = max(8, own)
    shared = part_v[pl.ds(pl.multiple_of(me * own // tile * tile, tile), tile), :]
    block = shared[:own]
    for i in range(1, tile // own):
        block = jnp.where(me % (tile // own) == i, shared[i * own:(i + 1) * own], block)
    for part in range(2):
        mine_of = block[:, part * stations:part * stations + share]
        for i in range(1, m):
            other = block[:, part * stations + i * share:part * stations + (i + 1) * share]
            mine_of = jnp.where(mine == i, other, mine_of)
        corr_ref[part] = mine_of

    sent = all_v.at[pl.ds(0, (n - 1) * rows)]
    pltpu.make_async_copy(sent, sent, send_sem).wait()


def solution(mesh):
    n, m = mesh.shape["sta"], mesh.shape["pt"]

    def body(greens, source_power, observed, pair_class, class_weight):
        own, pts = greens.shape[1], greens.shape[2]
        stations = own * n
        lanes = pts // 2 + 2 * stations
        any_space = pl.BlockSpec(memory_space=pl.ANY)
        vmem = pl.BlockSpec(memory_space=pltpu.VMEM)
        f32, bf16 = jnp.float32, jnp.bfloat16
        wide = (stations, 2 * stations)
        corr, grad = pl.pallas_call(
            functools.partial(kernel, n, m),
            out_shape=(
                jax.ShapeDtypeStruct((2, own, stations // m), f32),
                jax.ShapeDtypeStruct((1, pts), f32),
            ),
            in_specs=[any_space] * 5,
            out_specs=(vmem, vmem),
            scratch_shapes=[
                pltpu.VMEM(greens.shape, bf16),
                pltpu.VMEM((1, pts), f32),
                pltpu.VMEM(observed.shape, f32),
                pltpu.VMEM(pair_class.shape, jnp.int32),
                pltpu.SMEM(class_weight.shape, f32),
                pltpu.VMEM((n * own * 4, lanes), bf16),
                pltpu.VMEM((4, stations, pts // 2), bf16),
                pltpu.VMEM(wide, f32),
                pltpu.VMEM((m - 1,) + wide, f32),
                pltpu.VMEM(wide, f32),
                pltpu.VMEM(wide, f32),
                pltpu.SemaphoreType.DMA((5,)),
                pltpu.SemaphoreType.DMA,
                pltpu.SemaphoreType.DMA,
                pltpu.SemaphoreType.DMA((m - 1,)),
                pltpu.SemaphoreType.DMA((m - 1,)),
            ],
            compiler_params=pltpu.CompilerParams(
                collective_id=0, has_side_effects=True, vmem_limit_bytes=60 * 1024 * 1024
            ),
        )(greens, source_power[None], observed, pair_class, class_weight)
        return corr, grad[0]

    return jax.shard_map(
        body,
        mesh=mesh,
        in_specs=(P(None, "sta", "pt"), P("pt"), P(None, "sta", None), P("sta", None), P()),
        out_specs=(P(None, "sta", "pt"), P("pt")),
        check_vma=False,
    )
```

```python
import functools
import math

import jax
import jax.numpy as jnp
from jax import lax
from jax.experimental import pallas as pl
from jax.experimental.pallas import tpu as pltpu
from jax.sharding import PartitionSpec as P

CLASSES = 8
MESH = pl.DeviceIdType.MESH
UNROLL = 16


def each(first, last, step):
    if last - first <= UNROLL:
        for i in range(first, last):
            step(i)
    else:
        pl.loop(first, last)(step)


def kernel(
    n, m, greens_ref, power_ref, observed_ref, class_ref, weight_ref, corr_ref, grad_ref,
    greens_v, power_v, observed_v, class_v, weight_s, all_v, field_v, part_v, recv_v, gap_v, pair_v,
    in_sem, send_sem, recv_sem, pt_send, pt_recv,
):
    me, mine = lax.axis_index("sta"), lax.axis_index("pt")
    own, pts = greens_ref.shape[1], greens_ref.shape[2]
    stations = own * n
    half = pts // 2
    rows = 4 * own

    loads = [
        pltpu.make_async_copy(src, dst, in_sem.at[i])
        for i, (src, dst) in enumerate(
            ((greens_ref, greens_v), (observed_ref, observed_v), (class_ref, class_v),
             (power_ref, power_v), (weight_ref, weight_s))
        )
    ]
    for load in loads:
        load.start()

    barrier = pltpu.get_barrier_semaphore()

    def greet(i):
        pl.semaphore_signal(barrier, inc=1, device_id={"sta": lax.rem(me + i, n), "pt": mine}, device_id_type=MESH)

    def greet_pt(i):
        pl.semaphore_signal(barrier, inc=1, device_id={"sta": me, "pt": lax.rem(mine + i, m)}, device_id_type=MESH)

    each(1, n, greet)
    each(1, m, greet_pt)

    for load in loads[:3]:
        load.wait()
    g = greens_v[...].astype(jnp.float32)
    points = jnp.concatenate(
        [g[0, :, :half], g[1, :, :half], g[0, :, half:], g[1, :, half:]], axis=0
    ).astype(jnp.bfloat16)
    obs = jnp.concatenate([observed_v[0], observed_v[1]], axis=1)
    high = obs.astype(jnp.bfloat16).astype(jnp.float32)
    rest = obs - high
    mid = rest.astype(jnp.bfloat16).astype(jnp.float32)
    low = rest - mid
    cls = class_v[...].astype(jnp.float32)
    side = jnp.concatenate([high, mid, low, jnp.concatenate([cls, cls], axis=1)], axis=0).astype(jnp.bfloat16)
    here = all_v.at[pl.ds(pl.multiple_of(me * rows, rows), rows)]
    here[:, :half] = points
    here[:, half:] = side

    pl.semaphore_wait(barrier, (n - 1) + (m - 1))

    def send(i):
        pltpu.make_async_remote_copy(
            src_ref=here, dst_ref=here, send_sem=send_sem, recv_sem=recv_sem,
            device_id={"sta": lax.rem(me + i, n), "pt": mine}, device_id_type=MESH,
        ).start()

    each(1, n, send)

    group = math.gcd(n, 16)
    span = group * own
    size = group * rows
    at = lax.broadcasted_iota(jnp.int32, (size, size), 0)
    of = lax.broadcasted_iota(jnp.int32, (size, size), 1)
    source = (at % span) // own * rows + at // span * own + at % own
    order = jnp.where(of == source, 1.0, 0.0).astype(jnp.bfloat16)
    loads[3].wait()
    loads[4].wait()
    power = [power_v[:, :half], power_v[:, half:]]

    everything = all_v.at[pl.ds(0, (n - 1) * rows)]
    pltpu.make_async_copy(everything, everything, recv_sem).wait()

    def sort(b):
        block = all_v[pl.ds(pl.multiple_of(b * size, size), size), :]
        y = jnp.dot(order, block, preferred_element_type=jnp.float32)
        to = pl.ds(pl.multiple_of(b * span, span), span)
        for q in range(4):
            field_v[q, to, :] = y[q * span:(q + 1) * span, :half].astype(jnp.bfloat16)
        o = y[:, half:]
        gap_v[to, :] = o[:span] + o[span:2 * span] + o[2 * span:3 * span]
        c = o[3 * span:]
        total = jnp.zeros(c.shape, jnp.float32)
        for level in range(1, CLASSES):
            total = jnp.where(c == float(level), weight_s[level], total)
        row_ids = b * span + lax.broadcasted_iota(jnp.int32, c.shape, 0)
        col_ids = lax.broadcasted_iota(jnp.int32, c.shape, 1) % stations
        pair_v[to, :] = jnp.where(row_ids == col_ids, 0.0, total)

    each(0, n // group, sort)

    real, imag = (field_v[0], field_v[2]), (field_v[1], field_v[3])
    right = [
        jnp.concatenate([real[0], imag[0]], axis=0), jnp.concatenate([real[1], imag[1]], axis=0),
        jnp.concatenate([imag[0], -real[0]], axis=0), jnp.concatenate([imag[1], -real[1]], axis=0),
    ]
    right_real = jnp.concatenate([real[0], real[1], imag[0], imag[1]], axis=1)
    right_imag = jnp.concatenate([imag[0], imag[1], -real[0], -real[1]], axis=1)
    rights = jnp.concatenate([right_real, right_imag], axis=0)

    def correlate(b):
        to = pl.ds(pl.multiple_of(b * span, span), span)
        left = jnp.concatenate(
            [
                (power[h] * field_v[2 * h + part, to, :].astype(jnp.float32)).astype(jnp.bfloat16)
                for part in range(2) for h in range(2)
            ],
            axis=1,
        )
        part_v[to, :] = lax.dot_general(left, rights, (((1,), (1,)), ((), ())), preferred_element_type=jnp.float32)

    each(0, n // group, correlate)

    def exchange(i):
        return pltpu.make_async_remote_copy(
            src_ref=part_v, dst_ref=recv_v.at[i - 1], send_sem=pt_send.at[i - 1], recv_sem=pt_recv.at[i - 1],
            device_id={"sta": me, "pt": lax.rem(mine + i, m)}, device_id_type=MESH,
        )

    copies = [exchange(i) for i in range(1, m)]
    for copy in copies:
        copy.start()
    for copy in copies:
        copy.wait_recv()
    for copy in copies:
        copy.wait_send()

    scale = 1.0 / math.sqrt(pts * m)

    def adjoint(b, totals):
        to = pl.ds(pl.multiple_of(b * span, span), span)
        corr = part_v[to, :]
        for i in range(m - 1):
            corr = corr + recv_v[i, to, :]
        corr = corr * scale
        part_v[to, :] = corr
        a = (pair_v[to, :] * (corr - gap_v[to, :])).astype(jnp.bfloat16)
        out = []
        for h in range(2):
            field_real = jnp.dot(a, right[h], preferred_element_type=jnp.float32)
            field_imag = jnp.dot(a, right[2 + h], preferred_element_type=jnp.float32)
            term = (
                field_v[2 * h, to, :].astype(jnp.float32) * field_real
                + field_v[2 * h + 1, to, :].astype(jnp.float32) * field_imag
            )
            out.append(totals[h] + jnp.sum(term, axis=0, keepdims=True))
        return tuple(out)

    zero = jnp.zeros((1, half), jnp.float32)
    if n == group:
        totals = adjoint(0, (zero, zero))
    else:
        totals = lax.fori_loop(0, n // group, adjoint, (zero, zero))
    for h in range(2):
        grad_ref[:, h * half:(h + 1) * half] = totals[h] / stations

    share = stations // m
    tile = max(8, own)
    shared = part_v[pl.ds(pl.multiple_of(me * own // tile * tile, tile), tile), :]
    block = shared[:own]
    for i in range(1, tile // own):
        block = jnp.where(me % (tile // own) == i, shared[i * own:(i + 1) * own], block)
    for part in range(2):
        mine_of = block[:, part * stations:part * stations + share]
        for i in range(1, m):
            other = block[:, part * stations + i * share:part * stations + (i + 1) * share]
            mine_of = jnp.where(mine == i, other, mine_of)
        corr_ref[part] = mine_of

    sent = all_v.at[pl.ds(0, (n - 1) * rows)]
    pltpu.make_async_copy(sent, sent, send_sem).wait()


def hand_on(corr_ref, grad_ref, corr_out, grad_out, sems):
    copies = [
        pltpu.make_async_copy(corr_ref, corr_out, sems.at[0]),
        pltpu.make_async_copy(grad_ref, grad_out, sems.at[1]),
    ]
    for copy in copies:
        copy.start()
    for copy in copies:
        copy.wait()


def solution(mesh):
    n, m = mesh.shape["sta"], mesh.shape["pt"]

    def body(greens, source_power, observed, pair_class, class_weight):
        own, pts = greens.shape[1], greens.shape[2]
        stations = own * n
        lanes = pts // 2 + 2 * stations
        any_space = pl.BlockSpec(memory_space=pl.ANY)
        vmem = pl.BlockSpec(memory_space=pltpu.VMEM)
        f32, bf16 = jnp.float32, jnp.bfloat16
        wide = (stations, 2 * stations)
        corr, grad = pl.pallas_call(
            functools.partial(kernel, n, m),
            out_shape=(
                jax.ShapeDtypeStruct((2, own, stations // m), f32),
                jax.ShapeDtypeStruct((1, pts), f32),
            ),
            in_specs=[any_space] * 5,
            out_specs=(vmem, vmem),
            scratch_shapes=[
                pltpu.VMEM(greens.shape, bf16),
                pltpu.VMEM((1, pts), f32),
                pltpu.VMEM(observed.shape, f32),
                pltpu.VMEM(pair_class.shape, jnp.int32),
                pltpu.SMEM(class_weight.shape, f32),
                pltpu.VMEM((n * own * 4, lanes), bf16),
                pltpu.VMEM((4, stations, pts // 2), bf16),
                pltpu.VMEM(wide, f32),
                pltpu.VMEM((m - 1,) + wide, f32),
                pltpu.VMEM(wide, f32),
                pltpu.VMEM(wide, f32),
                pltpu.SemaphoreType.DMA((5,)),
                pltpu.SemaphoreType.DMA,
                pltpu.SemaphoreType.DMA,
                pltpu.SemaphoreType.DMA((m - 1,)),
                pltpu.SemaphoreType.DMA((m - 1,)),
            ],
            compiler_params=pltpu.CompilerParams(
                collective_id=0, has_side_effects=True, vmem_limit_bytes=60 * 1024 * 1024
            ),
        )(greens, source_power[None], observed, pair_class, class_weight)
        any_pair = (any_space, any_space)
        corr, grad = pl.pallas_call(
            hand_on,
            out_shape=(jax.ShapeDtypeStruct(corr.shape, f32), jax.ShapeDtypeStruct(grad.shape, f32)),
            in_specs=any_pair,
            out_specs=any_pair,
            scratch_shapes=[pltpu.SemaphoreType.DMA((2,))],
        )(corr, grad)
        return corr, grad[0]

    return jax.shard_map(
        body,
        mesh=mesh,
        in_specs=(P(None, "sta", "pt"), P("pt"), P(None, "sta", None), P("sta", None), P()),
        out_specs=(P(None, "sta", "pt"), P("pt")),
        check_vma=False,
    )
```

```python
import functools
import math

import jax
import jax.numpy as jnp
from jax import lax
from jax.experimental import pallas as pl
from jax.experimental.pallas import tpu as pltpu
from jax.sharding import PartitionSpec as P

CLASSES = 8
MESH = pl.DeviceIdType.MESH
UNROLL = 16


def each(first, last, step):
    if last - first <= UNROLL:
        for i in range(first, last):
            step(i)
    else:
        pl.loop(first, last)(step)


def kernel(
    n, m, greens_ref, power_ref, observed_ref, class_ref, weight_ref, corr_ref, grad_ref,
    greens_v, power_v, observed_v, class_v, weight_s, all_v, field_v, part_v, recv_v, gap_v, pair_v,
    in_sem, send_sem, recv_sem, pt_send, pt_recv,
):
    me, mine = lax.axis_index("sta"), lax.axis_index("pt")
    own, pts = greens_ref.shape[1], greens_ref.shape[2]
    stations = own * n
    half = pts // 2
    rows = 4 * own

    loads = [
        pltpu.make_async_copy(src, dst, in_sem.at[i])
        for i, (src, dst) in enumerate(
            ((greens_ref, greens_v), (observed_ref, observed_v), (class_ref, class_v),
             (power_ref, power_v), (weight_ref, weight_s))
        )
    ]
    for load in loads:
        load.start()

    barrier = pltpu.get_barrier_semaphore()

    def greet(i):
        pl.semaphore_signal(barrier, inc=1, device_id={"sta": i - 1 + jnp.where(i > me, 1, 0), "pt": mine}, device_id_type=MESH)

    def greet_pt(i):
        pl.semaphore_signal(barrier, inc=1, device_id={"sta": me, "pt": lax.rem(mine + i, m)}, device_id_type=MESH)

    each(1, n, greet)
    each(1, m, greet_pt)

    for load in loads[:3]:
        load.wait()
    g = greens_v[...].astype(jnp.float32)
    points = jnp.concatenate(
        [g[0, :, :half], g[1, :, :half], g[0, :, half:], g[1, :, half:]], axis=0
    ).astype(jnp.bfloat16)
    obs = jnp.concatenate([observed_v[0], observed_v[1]], axis=1)
    high = obs.astype(jnp.bfloat16).astype(jnp.float32)
    rest = obs - high
    mid = rest.astype(jnp.bfloat16).astype(jnp.float32)
    low = rest - mid
    cls = class_v[...].astype(jnp.float32)
    side = jnp.concatenate([high, mid, low, jnp.concatenate([cls, cls], axis=1)], axis=0).astype(jnp.bfloat16)
    here = all_v.at[pl.ds(pl.multiple_of(me * rows, rows), rows)]
    here[:, :half] = points
    here[:, half:] = side

    pl.semaphore_wait(barrier, (n - 1) + (m - 1))

    def send(i):
        pltpu.make_async_remote_copy(
            src_ref=here, dst_ref=here, send_sem=send_sem, recv_sem=recv_sem,
            device_id={"sta": i - 1 + jnp.where(i > me, 1, 0), "pt": mine}, device_id_type=MESH,
        ).start()

    each(1, n, send)

    group = math.gcd(n, 16)
    span = group * own
    size = group * rows
    at = lax.broadcasted_iota(jnp.int32, (size, size), 0)
    of = lax.broadcasted_iota(jnp.int32, (size, size), 1)
    source = (at % span) // own * rows + at // span * own + at % own
    order = jnp.where(of == source, 1.0, 0.0).astype(jnp.bfloat16)
    loads[3].wait()
    loads[4].wait()
    power = [power_v[:, :half], power_v[:, half:]]

    everything = all_v.at[pl.ds(0, (n - 1) * rows)]
    pltpu.make_async_copy(everything, everything, recv_sem).wait()

    def sort(b):
        block = all_v[pl.ds(pl.multiple_of(b * size, size), size), :]
        y = jnp.dot(order, block[:, :half], preferred_element_type=jnp.float32)
        to = pl.ds(pl.multiple_of(b * span, span), span)
        for q in range(4):
            field_v[q, to, :] = y[q * span:(q + 1) * span].astype(jnp.bfloat16)

    each(0, n // group, sort)

    real, imag = (field_v[0], field_v[2]), (field_v[1], field_v[3])
    right = [
        jnp.concatenate([real[0], imag[0]], axis=0), jnp.concatenate([real[1], imag[1]], axis=0),
        jnp.concatenate([imag[0], -real[0]], axis=0), jnp.concatenate([imag[1], -real[1]], axis=0),
    ]
    right_real = jnp.concatenate([real[0], real[1], imag[0], imag[1]], axis=1)
    right_imag = jnp.concatenate([imag[0], imag[1], -real[0], -real[1]], axis=1)
    rights = jnp.concatenate([right_real, right_imag], axis=0)

    def correlate(b):
        to = pl.ds(pl.multiple_of(b * span, span), span)
        left = jnp.concatenate(
            [
                (power[h] * field_v[2 * h + part, to, :].astype(jnp.float32)).astype(jnp.bfloat16)
                for part in range(2) for h in range(2)
            ],
            axis=1,
        )
        part_v[to, :] = lax.dot_general(left, rights, (((1,), (1,)), ((), ())), preferred_element_type=jnp.float32)

    each(0, n // group, correlate)

    def exchange(i):
        return pltpu.make_async_remote_copy(
            src_ref=part_v, dst_ref=recv_v.at[i - 1], send_sem=pt_send.at[i - 1], recv_sem=pt_recv.at[i - 1],
            device_id={"sta": me, "pt": lax.rem(mine + i, m)}, device_id_type=MESH,
        )

    copies = [exchange(i) for i in range(1, m)]
    for copy in copies:
        copy.start()
    def sort_side(b):
        block = all_v[pl.ds(pl.multiple_of(b * size, size), size), half:]
        o = jnp.dot(order, block, preferred_element_type=jnp.float32)
        to = pl.ds(pl.multiple_of(b * span, span), span)
        gap_v[to, :] = o[:span] + o[span:2 * span] + o[2 * span:3 * span]
        c = o[3 * span:]
        total = jnp.zeros(c.shape, jnp.float32)
        for level in range(1, CLASSES):
            total = jnp.where(c == float(level), weight_s[level], total)
        row_ids = b * span + lax.broadcasted_iota(jnp.int32, c.shape, 0)
        col_ids = lax.broadcasted_iota(jnp.int32, c.shape, 1) % stations
        pair_v[to, :] = jnp.where(row_ids == col_ids, 0.0, total)

    each(0, n // group, sort_side)

    for copy in copies:
        copy.wait_recv()

    scale = 1.0 / math.sqrt(pts * m)

    def adjoint(b, totals):
        to = pl.ds(pl.multiple_of(b * span, span), span)
        corr = part_v[to, :]
        for i in range(m - 1):
            corr = corr + recv_v[i, to, :]
        corr = corr * scale
        a = (pair_v[to, :] * (corr - gap_v[to, :])).astype(jnp.bfloat16)
        gap_v[to, :] = corr
        out = []
        for h in range(2):
            field_real = jnp.dot(a, right[h], preferred_element_type=jnp.float32)
            field_imag = jnp.dot(a, right[2 + h], preferred_element_type=jnp.float32)
            term = (
                field_v[2 * h, to, :].astype(jnp.float32) * field_real
                + field_v[2 * h + 1, to, :].astype(jnp.float32) * field_imag
            )
            out.append(totals[h] + jnp.sum(term, axis=0, keepdims=True))
        return tuple(out)

    zero = jnp.zeros((1, half), jnp.float32)
    if n == group:
        totals = adjoint(0, (zero, zero))
    else:
        totals = lax.fori_loop(0, n // group, adjoint, (zero, zero))
    for h in range(2):
        grad_ref[:, h * half:(h + 1) * half] = totals[h] / stations

    share = stations // m
    tile = max(8, own)
    shared = gap_v[pl.ds(pl.multiple_of(me * own // tile * tile, tile), tile), :]
    block = shared[:own]
    for i in range(1, tile // own):
        block = jnp.where(me % (tile // own) == i, shared[i * own:(i + 1) * own], block)
    for part in range(2):
        mine_of = block[:, part * stations:part * stations + share]
        for i in range(1, m):
            other = block[:, part * stations + i * share:part * stations + (i + 1) * share]
            mine_of = jnp.where(mine == i, other, mine_of)
        corr_ref[part] = mine_of

    for copy in copies:
        copy.wait_send()
    sent = all_v.at[pl.ds(0, (n - 1) * rows)]
    pltpu.make_async_copy(sent, sent, send_sem).wait()


def hand_on(corr_ref, grad_ref, corr_out, grad_out, sems):
    copies = [
        pltpu.make_async_copy(corr_ref, corr_out, sems.at[0]),
        pltpu.make_async_copy(grad_ref, grad_out, sems.at[1]),
    ]
    for copy in copies:
        copy.start()
    for copy in copies:
        copy.wait()


def solution(mesh):
    n, m = mesh.shape["sta"], mesh.shape["pt"]

    def body(greens, source_power, observed, pair_class, class_weight):
        own, pts = greens.shape[1], greens.shape[2]
        stations = own * n
        lanes = pts // 2 + 2 * stations
        any_space = pl.BlockSpec(memory_space=pl.ANY)
        vmem = pl.BlockSpec(memory_space=pltpu.VMEM)
        f32, bf16 = jnp.float32, jnp.bfloat16
        wide = (stations, 2 * stations)
        corr, grad = pl.pallas_call(
            functools.partial(kernel, n, m),
            out_shape=(
                jax.ShapeDtypeStruct((2, own, stations // m), f32),
                jax.ShapeDtypeStruct((1, pts), f32),
            ),
            in_specs=[any_space] * 5,
            out_specs=(vmem, vmem),
            scratch_shapes=[
                pltpu.VMEM(greens.shape, bf16),
                pltpu.VMEM((1, pts), f32),
                pltpu.VMEM(observed.shape, f32),
                pltpu.VMEM(pair_class.shape, jnp.int32),
                pltpu.SMEM(class_weight.shape, f32),
                pltpu.VMEM((n * own * 4, lanes), bf16),
                pltpu.VMEM((4, stations, pts // 2), bf16),
                pltpu.VMEM(wide, f32),
                pltpu.VMEM((m - 1,) + wide, f32),
                pltpu.VMEM(wide, f32),
                pltpu.VMEM(wide, f32),
                pltpu.SemaphoreType.DMA((5,)),
                pltpu.SemaphoreType.DMA,
                pltpu.SemaphoreType.DMA,
                pltpu.SemaphoreType.DMA((m - 1,)),
                pltpu.SemaphoreType.DMA((m - 1,)),
            ],
            compiler_params=pltpu.CompilerParams(
                collective_id=0, has_side_effects=True, vmem_limit_bytes=60 * 1024 * 1024
            ),
        )(greens, source_power[None], observed, pair_class, class_weight)
        any_pair = (any_space, any_space)
        corr, grad = pl.pallas_call(
            hand_on,
            out_shape=(jax.ShapeDtypeStruct(corr.shape, f32), jax.ShapeDtypeStruct(grad.shape, f32)),
            in_specs=any_pair,
            out_specs=any_pair,
            scratch_shapes=[pltpu.SemaphoreType.DMA((2,))],
        )(corr, grad)
        return corr, grad[0]

    return jax.shard_map(
        body,
        mesh=mesh,
        in_specs=(P(None, "sta", "pt"), P("pt"), P(None, "sta", None), P("sta", None), P()),
        out_specs=(P(None, "sta", "pt"), P("pt")),
        check_vma=False,
    )
```
